256 devices in a mesh: dp: 8 (over z), expert: 32 (over y, x, core).
Axes of the slice: x: 4, y: 4, z: 8, core: 2. Of those that a mesh axis runs over, the one named last changes fastest.
Arguments:
- tokens: bfloat16 [32768, 2048], P(('dp', 'expert')), may hold values from -6 to 6
- layer_output_gradient: bfloat16 [32768, 2048], P(('dp', 'expert')), may hold values from -24 to 24
- routes: int32 [32768, 8], P(('dp', 'expert')), may hold values from 0 to 63, all different within a row; in each aligned block of 128 rows (0 to 127, 128 to 255, ...) at most 18 rows name the same one
- routing_weight: bfloat16 [32768, 8], P(('dp', 'expert')), may hold values from 0.019897461 to 0.5
- tenant: int32 [32768], P(('dp', 'expert')), may hold values from 0 to 7, never falling along the last dimension, each value on 1 to 8192 neighbouring positions
- gate_weight: bfloat16 [64, 2048, 384], P('expert'), may hold values from -0.125 to 0.125
- up_weight: bfloat16 [64, 2048, 384], P('expert'), may hold values from -0.125 to 0.125
- down_weight: bfloat16 [64, 384, 2048], P('expert'), may hold values from -0.3125 to 0.3125
- adapter_input_maps: bfloat16 [64, 384, 128], P('expert'), may hold values from -0.3125 to 0.3125
- adapter_output_maps: bfloat16 [64, 128, 2048], P('expert'), may hold values from -0.125 to 0.125
Outputs:
- grad_tokens: bfloat16 [32768, 2048], P(('dp', 'expert'))
- adapter_input_gradient: float32 [64, 384, 128], P('expert')
- adapter_output_gradient: float32 [64, 128, 2048], P('expert', None, 'dp')
The draws below stay inside these ranges and needn't reach their ends.
Inputs may be any that keep to these rules, and one draw needn't show every extreme that they name: `routes`: each row names 8 different experts. Within the 128 rows of one device no expert is named more than 18 times, and in some devices' rows some expert is named exactly 18 times. Tenant ids never fall along the tokens; every tenant holds at least one token and at most 8192 tokens, and one tenant holds exactly that many.
All inputs are finite; a program needn't handle non-finite values.
Results may differ from the reference program's by a relative error of at most 0.0064.
Values may be sent and summed in bfloat16 or wider, within the bound.
No kernel may reach another device: no remote copies, remote signals or barrier semaphores. Data moves between devices by JAX's collectives and lax.ppermute only.
A program may use at most 128 MiB of HBM per device.

```python
import math
import jax
import jax.numpy as jnp
import numpy as np
from jax import lax

MODEL_WIDTH = 2048
HIDDEN_UNITS = 384
TOP = 8
ADAPTER_RANK = 16
TENANTS = 8
TOK_DEV = 128
EXPERT_COUNT = 64
TENANT_COLUMNS = 128
CAP = 18
GROUP_TOK = 4096
TOKENS = 32768
N_DP = 8
N_EXPERT = 32


def with_spikes(values, own_key, source, target, shards_of, factor):
    owner, partner = [(jnp.arange(values.shape[dim]) // (values.shape[dim] // shards_of)).reshape([-1 if axis == dim else 1 for axis in range(values.ndim)]) for dim in (source, target)]
    chosen = jax.random.permutation(own_key, shards_of)[partner]
    strong = (owner == chosen) | (owner == (partner + shards_of // 2) % shards_of)
    return jnp.where(strong, factor * values, values)


def block_scale(stream_key, dims, cuts, least, top_value):
    def one(axis_at, shards_of):
        heights = jax.random.uniform(jax.random.fold_in(jax.random.fold_in(stream_key, 6), axis_at), (shards_of,), jnp.float32, least / len(cuts), top_value / len(cuts))
        return jnp.repeat(jnp.exp(heights), dims[axis_at] // shards_of).reshape((-1,) + (1,) * (len(dims) - axis_at - 1))

    factor_of = one(*cuts[0])
    for cut in cuts[1:]:
        factor_of = factor_of * one(*cut)
    return factor_of


def length_profile(count, total, bound, slope):
    portions = [(1 << 20) // math.isqrt(standing ** slope) + 1 for standing in range(2, count + 1)]
    surplus, counts = total - bound - (count - 1), [1] * (count - 1)
    while surplus > 0:
        candidates = [i for i in range(count - 1) if counts[i] < bound]
        mass, left = sum([portions[i] for i in candidates]), surplus
        for i in candidates:
            more = min(bound - counts[i], max(1, left * portions[i] // mass), surplus)
            counts[i] = counts[i] + more
            surplus = surplus - more
    return np.array([bound] + counts)


def ragged_sizes(key, amount, total, most, lean):
    if amount == 2:
        one = jax.random.randint(key, (), max(1, total - most), min(most, total - 1) + 1)
        return jnp.stack([one, total - one])
    sizes = jnp.asarray(length_profile(amount, total, most, lean), jnp.int32)
    pairs = (amount - 1) // 2
    source_of, taker = sizes[1:1 + 2 * pairs:2], sizes[2:2 + 2 * pairs:2]
    room = jnp.minimum(source_of - 1, most - taker)
    passed = jax.random.randint(jax.random.fold_in(key, 1), (pairs,), 0, 1 << 20) % (room + 1)
    sizes = sizes.at[1:1 + 2 * pairs:2].set(source_of - passed).at[2:2 + 2 * pairs:2].set(taker + passed)
    return sizes[jax.random.permutation(jax.random.fold_in(key, 2), amount)]


def routed_block(own_key, own, number, rows, number_of, top, most, skew):
    ranking = jax.random.permutation(own_key, number_of)
    heavy_load, common = portions_of(number_of, rows * top, most, skew, True), portions_of(number_of, rows * top, most, skew, False)
    places = jnp.arange(number_of)

    def named(tallies, rotation):
        used = int((tallies > 0).sum())
        fixed = max(1, used // 4)
        shifted = fixed + (places - fixed + rotation * (used - fixed)) % max(1, number_of - fixed)
        return jnp.zeros((number_of,), jnp.int32).at[ranking[jnp.where(places < fixed, places, shifted)]].set(jnp.asarray(tallies, jnp.int32))

    tallies = jnp.where(number % 4 == 0, named(heavy_load, number // 4), named(common, number - number // 4 - 1))
    mixed = jax.random.permutation(jax.random.fold_in(own, 3), number_of)
    source_of, taker = mixed[0:number_of // 2 * 2:2], mixed[1:number_of // 2 * 2:2]
    room = jnp.minimum(tallies[source_of] - 1, most - tallies[taker]) // 2
    room = jnp.where((source_of == ranking[0]) | (taker == ranking[0]) | (tallies[taker] == 0), 0, jnp.maximum(room, 0))
    shifted = jax.random.randint(jax.random.fold_in(own, 4), (number_of // 2,), 0, 1 << 20) % (room + 1)
    tallies = tallies.at[source_of].add(-shifted).at[taker].add(shifted)
    labels = jnp.searchsorted(jnp.cumsum(tallies), jnp.arange(rows * top), side="right").astype(jnp.int32)
    table = labels.reshape(top, rows).T
    table = table[jax.random.permutation(jax.random.fold_in(own, 1), rows)]
    rotation = jax.random.randint(jax.random.fold_in(own, 2), (rows, 1), 0, top)
    return jnp.take_along_axis(table, (jnp.arange(top)[None, :] + rotation) % top, axis=1)


def portions_of(amount, total, bound, lean, full):
    portions = [(1 << 20) // math.isqrt(grade ** lean) + 1 for grade in range(1, amount + 1)]
    largest = bound if full else min(bound, max(-(-total // amount), total * portions[0] // sum(portions)))
    least = 1 if total - largest >= amount - 1 else 0
    given, surplus = [largest] + [least] * (amount - 1), total - largest - least * (amount - 1)
    while surplus > 0:
        movable = [i for i in range(1, amount) if given[i] < largest] or [i for i in range(1, amount) if given[i] < bound]
        whole, remaining = sum([portions[i] for i in movable]), surplus
        for i in movable:
            extra = min(bound - given[i], max(1, remaining * portions[i] // whole), surplus)
            given[i] = given[i] + extra
            surplus = surplus - extra
    return np.array(given)


def scatter_about(own_key, shape, spread, reach, pieces=(), kind=jnp.bfloat16):
    entries = jax.random.normal(own_key, shape, jnp.float32) * spread
    if len(pieces) > 0:
        entries = block_scale(own_key, shape, pieces, -0.22, 0.18) * entries
    return jnp.clip(entries, min=-reach, max=reach).astype(kind)


def bell_draw_with(key, shape, spread, most, pieces, heavy, held_as=jnp.bfloat16):
    entries = spread * jax.random.normal(key, shape, jnp.float32)
    if pieces:
        entries = entries * block_scale(key, shape, pieces, -0.22, 0.18)
    return jnp.clip(with_spikes(entries, jax.random.fold_in(key, 3), *heavy), -most, most).astype(held_as)


def setup_inputs(seed: int = 0) -> dict:
    arg_keys = jax.random.split(jax.random.key(seed), 11)
    tokens = scatter_about(arg_keys[0], (TOKENS, MODEL_WIDTH), 1.0, 6.0, ((0, 256),))
    layer_output_gradient = bell_draw_with(arg_keys[1], (TOKENS, MODEL_WIDTH), 1.0, 24.0, ((0, 256),), (0, 1, 256, 6.0))
    routes_keys = jax.random.split(jax.random.fold_in(arg_keys[2], 1), TOKENS // TOK_DEV)
    routes_turns = jax.random.permutation(jax.random.fold_in(arg_keys[2], 3), TOKENS // TOK_DEV)
    routes = jax.vmap(lambda own, number: routed_block(jax.random.fold_in(arg_keys[2], 2), own, number, TOK_DEV, EXPERT_COUNT, TOP, CAP, 2))(routes_keys, routes_turns).reshape((TOKENS, TOP))
    routing_weight = jnp.clip(jnp.exp(math.log(0.5) - 3.224016 * jax.random.uniform(arg_keys[3], (TOKENS, TOP), jnp.float32) ** block_scale(arg_keys[3], (TOKENS, TOP), ((0, 256),), -0.2, 0.2)), 0.019897461, 0.5).astype(jnp.bfloat16)
    tenant = jnp.searchsorted(jnp.cumsum(ragged_sizes(arg_keys[4], TENANTS, TOKENS, 2 * GROUP_TOK, 1)), jnp.arange(TOKENS), side="right").astype(jnp.int32)
    gate_weight = scatter_about(arg_keys[5], (EXPERT_COUNT, MODEL_WIDTH, HIDDEN_UNITS), MODEL_WIDTH ** -0.5, 0.125, ((0, 32),))
    up_weight = scatter_about(arg_keys[6], (EXPERT_COUNT, MODEL_WIDTH, HIDDEN_UNITS), MODEL_WIDTH ** -0.5, 0.125, ((0, 32),))
    down_weight = scatter_about(arg_keys[7], (EXPERT_COUNT, HIDDEN_UNITS, MODEL_WIDTH), HIDDEN_UNITS ** -0.5, 0.3125, ((0, 32),))
    adapter_input_maps = scatter_about(arg_keys[8], (EXPERT_COUNT, HIDDEN_UNITS, TENANT_COLUMNS), HIDDEN_UNITS ** -0.5, 0.3125, ((0, 32),))
    adapter_output_maps = scatter_about(arg_keys[9], (EXPERT_COUNT, TENANT_COLUMNS, MODEL_WIDTH), MODEL_WIDTH ** -0.5, 0.125, ((0, 32),))
    return {"tokens": tokens, "layer_output_gradient": layer_output_gradient, "routes": routes, "routing_weight": routing_weight, "tenant": tenant, "gate_weight": gate_weight, "up_weight": up_weight, "down_weight": down_weight, "adapter_input_maps": adapter_input_maps, "adapter_output_maps": adapter_output_maps}


def expert_gradients(input_rows, scaled_rows, token_mask, gate_w, up_w, down_w, low_a, low_b):
    gate = jnp.dot(input_rows, gate_w, preferred_element_type=jnp.float32)
    upper = jnp.dot(input_rows, up_w, preferred_element_type=jnp.float32)
    sigma = jax.nn.sigmoid(gate)
    active = gate * sigma
    hidden_units = (active * upper).astype(jnp.bfloat16)
    low = (jnp.dot(hidden_units, low_a, preferred_element_type=jnp.float32) * token_mask).astype(jnp.bfloat16)
    backward_adapter = (jnp.dot(scaled_rows, low_b.T, preferred_element_type=jnp.float32) * token_mask).astype(jnp.bfloat16)
    output_map_gradient = jnp.dot(low.T, scaled_rows, preferred_element_type=jnp.float32)
    input_map_gradient = jnp.dot(hidden_units.T, backward_adapter, preferred_element_type=jnp.float32)
    hidden_gradient = jnp.dot(scaled_rows, down_w.T, preferred_element_type=jnp.float32) + jnp.dot(backward_adapter, low_a.T, preferred_element_type=jnp.float32)
    dgate = (hidden_gradient * upper * sigma * (1.0 + gate * (1.0 - sigma))).astype(jnp.bfloat16)
    dupper = (hidden_gradient * active).astype(jnp.bfloat16)
    backward_pass = jnp.dot(dgate, gate_w.T, preferred_element_type=jnp.float32) + jnp.dot(dupper, up_w.T, preferred_element_type=jnp.float32)
    return backward_pass.astype(jnp.bfloat16), input_map_gradient, output_map_gradient


def reference(tokens, layer_output_gradient, routes, routing_weight, tenant, gate_weight, up_weight, down_weight, adapter_input_maps, adapter_output_maps):
    total = TOKENS * TOP
    most_rows = N_DP * N_EXPERT * CAP
    flat_routes = routes.reshape(-1)
    flat_weights = routing_weight.reshape(-1).astype(jnp.float32)
    column_span = jnp.arange(TENANTS * ADAPTER_RANK, dtype=jnp.int32) // ADAPTER_RANK

    def single_expert(carry, expert_index):
        picked = jnp.nonzero(flat_routes == expert_index, size=most_rows, fill_value=total)[0].astype(jnp.int32)
        valid = picked < total
        safe = jnp.where(valid, picked, 0).astype(jnp.int32)
        tok_rows = (safe // TOP).astype(jnp.int32)
        weight = jnp.where(valid, flat_weights[safe], jnp.zeros_like(flat_weights[safe]))
        input_rows = tokens[tok_rows]
        scaled_rows = (weight[:, None] * layer_output_gradient[tok_rows].astype(jnp.float32)).astype(jnp.bfloat16)
        token_mask = (column_span[None, :] == tenant[tok_rows][:, None]).astype(jnp.float32)
        backward_pass, input_map_gradient, output_map_gradient = expert_gradients(input_rows, scaled_rows, token_mask, gate_weight[expert_index], up_weight[expert_index], down_weight[expert_index], adapter_input_maps[expert_index], adapter_output_maps[expert_index])
        carry = carry.at[tok_rows].add(backward_pass.astype(jnp.float32))
        return carry, (input_map_gradient, output_map_gradient)

    start_column = jnp.zeros((TOKENS, MODEL_WIDTH), jnp.float32)
    summed_rows, (adapter_input_gradient, adapter_output_gradient) = lax.scan(single_expert, start_column, jnp.arange(EXPERT_COUNT, dtype=jnp.int32))
    return summed_rows.astype(jnp.bfloat16), adapter_input_gradient, adapter_output_gradient
```

```python
import jax
import jax.numpy as jnp
from jax import lax
from jax.experimental import pallas as pl
from jax.experimental.pallas import tpu as pltpu
from jax.sharding import PartitionSpec as P

SIDE = 4
TOK = 128
WIDTH = 2048
HID = 384
COLS = 128
RANK = 16
TOP = 8
CAP = 18
EXPERTS = 64
META = 128
WIDE = WIDTH + META
LINE = SIDE * TOK
USED = SIDE * CAP
PITCH = 80
DESTS = ((0, 0), (0, 1), (1, 0), (3, 0), (1, 1), (3, 1), (2, 0), (2, 1))
NB = len(DESTS)
BF = jnp.bfloat16
F32 = jnp.float32
MIB = 1024 * 1024


def place(y, x, c):
    return ((y % SIDE) * SIDE + x % SIDE) * 2 + c


def all_places():
    return [(y, x, c) for y in range(SIDE) for x in range(SIDE) for c in range(2)]


def line_pairs(d):
    return [
        (place(y, x, c), place(y + d, x, c) if c == 0 else place(y, x + d, c))
        for y, x, c in all_places()
    ]


def cross_pairs(d, other):
    return [
        (place(y, x, c), place(y, x + d, c ^ other) if c == 0 else place(y + d, x, c ^ other))
        for y, x, c in all_places()
    ]


def back_pairs(pairs):
    return [(b, a) for a, b in pairs]


def params(mib, dims=0):
    return pltpu.CompilerParams(
        vmem_limit_bytes=mib * MIB,
        dimension_semantics=("arbitrary",) * dims if dims else None,
    )


def cost(flops, nbytes):
    return pl.CostEstimate(flops=flops, bytes_accessed=nbytes, transcendentals=0)


def iota(shape, dim):
    return lax.broadcasted_iota(jnp.int32, shape, dim)


def dot(a, b, ca=1, cb=0):
    return lax.dot_general(a, b, (((ca,), (cb,)), ((), ())), preferred_element_type=F32)


def build_onehots(metas, o_ref, ow_ref):
    me = lax.axis_index("expert")
    c, x, y = me & 1, (me >> 1) & 3, me >> 3
    ids = iota((EXPERTS, TOK), 0).astype(F32)
    tri = (iota((TOK, TOK), 0) <= iota((TOK, TOK), 1)).astype(F32).astype(BF)
    ranks, weights = [], []
    for meta in metas:
        flipped = meta.astype(F32).T
        named = jnp.zeros((EXPERTS, TOK), F32)
        weight = jnp.zeros((EXPERTS, TOK), F32)
        for k in range(TOP):
            hit = flipped[k : k + 1, :] == ids
            named = named + jnp.where(hit, 1.0, 0.0)
            weight = weight + jnp.where(hit, flipped[TOP + k : TOP + k + 1, :], 0.0)
        rank = dot(named.astype(BF), tri) * named
        ranks.append(rank.astype(BF))
        weights.append(weight.astype(BF))
    rank = jnp.concatenate(ranks, axis=1)
    weight = jnp.concatenate(weights, axis=1)
    rows = 2 * PITCH
    r = iota((rows, LINE), 0)
    j = (r >= PITCH).astype(jnp.int32)
    rr = r - PITCH * j
    d = sum((rr >= CAP * i).astype(jnp.int32) for i in range(1, SIDE))
    want = jnp.where((rr < USED) & ((iota((rows, LINE), 1) >> 7) == d), rr - CAP * d + 1, -1)
    want = want.astype(F32)
    col = iota((rows, EXPERTS), 1) - (iota((rows, EXPERTS), 0) >= PITCH).astype(jnp.int32)
    for b, (step, other) in enumerate(DESTS):
        along_x = (y << 4) + (((x + step) & 3) << 2)
        along_y = (((y + step) & 3) << 4) + (x << 2)
        base = jnp.where(c == 0, along_x, along_y) + ((c ^ other) << 1)
        sel = (col == base).astype(F32).astype(BF)
        hit = dot(sel, rank) == want
        o_ref[b * rows : (b + 1) * rows, :] = jnp.where(hit, 1.0, 0.0).astype(BF)
        ow_ref[b * rows : (b + 1) * rows, :] = jnp.where(hit, dot(sel, weight), 0.0).astype(BF)


def pick_rows(o, xs_ref, outs, start, size):
    picked = dot(o, xs_ref[:, pl.ds(start, size)])
    for b in range(NB):
        for j in range(2):
            at = (2 * b + j) * PITCH
            outs[b][j, :, pl.ds(start, size)] = picked[at : at + USED].astype(BF)


def gather_x_kernel(x0, x1, x2, x3, o_ref, ow_ref, *rest):
    outs, xs_ref = rest[:NB], rest[NB]
    metas = []
    for i, x in enumerate((x0, x1, x2, x3)):
        xs_ref[i * TOK : (i + 1) * TOK, :] = x[...]
        metas.append(x[:, WIDTH:])
    build_onehots(metas, o_ref, ow_ref)

    def step(n, carry):
        pick_rows(o_ref[...], xs_ref, outs, pl.multiple_of(n * 256, 256), 256)
        return carry

    lax.fori_loop(0, WIDTH // 256, step, 0)
    pick_rows(o_ref[...], xs_ref, outs, WIDTH, META)


def gather_dy_kernel(ow_ref, y0, y1, y2, y3, *rest):
    outs, ys_ref = rest[:NB], rest[NB]
    for i, y in enumerate((y0, y1, y2, y3)):
        ys_ref[i * TOK : (i + 1) * TOK, :] = y[...]

    def step(n, carry):
        pick_rows(ow_ref[...], ys_ref, outs, pl.multiple_of(n * 256, 256), 256)
        return carry

    lax.fori_loop(0, WIDTH // 256, step, 0)


def gather_x(blocks):
    onehot = jax.ShapeDtypeStruct((NB * 2 * PITCH, LINE), BF)
    out = jax.ShapeDtypeStruct((2, USED, WIDE), BF)
    res = pl.pallas_call(
        gather_x_kernel,
        out_shape=(onehot, onehot) + (out,) * NB,
        scratch_shapes=[pltpu.VMEM((LINE, WIDE), BF)],
        compiler_params=params(40),
        cost_estimate=cost(4 * 10**9, 12 * 10**6),
        name="gather_x",
    )(*blocks)
    return res[0], res[1], res[2:]


def gather_dy(onehot, blocks):
    return pl.pallas_call(
        gather_dy_kernel,
        out_shape=(jax.ShapeDtypeStruct((2, USED, WIDTH), BF),) * NB,
        scratch_shapes=[pltpu.VMEM((LINE, WIDTH), BF)],
        compiler_params=params(40),
        cost_estimate=cost(4 * 10**9, 12 * 10**6),
        name="gather_dy",
    )(onehot, *blocks)


def per_expert(shape):
    return pl.BlockSpec((1,) + shape, lambda j: (j, 0, 0))


def stack(scratch, blocks, width):
    @pl.when(pl.program_id(0) == 0)
    def _():
        scratch[...] = jnp.zeros_like(scratch)

    for i, block in enumerate(blocks):
        scratch[i * PITCH : i * PITCH + USED, :] = block[0, :, :width]


def forward_kernel(*refs):
    blocks, (wg, wu, a, hid, low, mask, a1, a2, xs, ts) = refs[:NB], refs[NB:]
    stack(xs, blocks, WIDTH)
    for i, block in enumerate(blocks):
        ts[i * PITCH : i * PITCH + USED, :] = block[0, :, WIDTH:].astype(F32)
    x = xs[...]
    gate = dot(x, wg[0])
    up = dot(x, wu[0])
    sig = jax.nn.sigmoid(gate)
    act = gate * sig
    h = (act * up).astype(BF)
    hid[0] = h
    a1[0] = up * sig * (1.0 + gate * (1.0 - sig))
    a2[0] = act
    tenant = ts[:, 2 * TOP : 2 * TOP + 1]
    column = (iota((NB * PITCH, COLS), 1) >> 4).astype(F32)
    m = jnp.where(tenant == column, 1.0, 0.0)
    mask[0] = m.astype(BF)
    low[0] = (dot(h, a[0]) * m).astype(BF)


def forward(blocks, wg, wu, a):
    rows = NB * PITCH
    sds = jax.ShapeDtypeStruct
    return pl.pallas_call(
        forward_kernel,
        grid=(2,),
        in_specs=[per_expert((USED, WIDE))] * NB
        + [per_expert((WIDTH, HID)), per_expert((WIDTH, HID)), per_expert((HID, COLS))],
        out_specs=[
            per_expert((rows, HID)),
            per_expert((rows, COLS)),
            per_expert((rows, COLS)),
            per_expert((rows, HID)),
            per_expert((rows, HID)),
        ],
        out_shape=(
            sds((2, rows, HID), BF),
            sds((2, rows, COLS), BF),
            sds((2, rows, COLS), BF),
            sds((2, rows, HID), F32),
            sds((2, rows, HID), F32),
        ),
        scratch_shapes=[pltpu.VMEM((rows, WIDTH), BF), pltpu.VMEM((rows, COLS), F32)],
        compiler_params=params(48, 1),
        cost_estimate=cost(5 * 10**9, 18 * 10**6),
        name="forward",
    )(*blocks, wg, wu, a)


def backward_kernel(n, *refs):
    blocks, (wd, bm, a, wg, wu, mask, a1, a2) = refs[:n], refs[n : n + 8]
    outs, (back_low, ys) = refs[n + 8 : 2 * n + 8], refs[2 * n + 8 :]
    stack(ys, blocks, WIDTH)
    s = ys[...]
    bl = (dot(s, bm[0], 1, 1) * mask[0].astype(F32)).astype(BF)
    back_low[0] = bl
    dh = dot(s, wd[0], 1, 1) + dot(bl, a[0], 1, 1)
    dgate = (dh * a1[0]).astype(BF)
    dup = (dh * a2[0]).astype(BF)
    for k in range(WIDTH // 512):
        at = slice(k * 512, (k + 1) * 512)
        back = dot(dgate, wg[0, at, :], 1, 1) + dot(dup, wu[0, at, :], 1, 1)
        for i in range(n):
            outs[i][0, :, at] = back[i * PITCH : i * PITCH + USED].astype(BF)


def backward(part, blocks, wd, bm, a, wg, wu, mask, a1, a2):
    n = len(blocks)
    rows = n * PITCH

    def half(cols):
        return pl.BlockSpec((1, rows, cols), lambda j: (j, part, 0))

    res = pl.pallas_call(
        lambda *refs: backward_kernel(n, *refs),
        grid=(2,),
        in_specs=[per_expert((USED, WIDTH))] * n
        + [
            per_expert((HID, WIDTH)),
            per_expert((COLS, WIDTH)),
            per_expert((HID, COLS)),
            per_expert((WIDTH, HID)),
            per_expert((WIDTH, HID)),
            half(COLS),
            half(HID),
            half(HID),
        ],
        out_specs=[per_expert((USED, WIDTH))] * n + [per_expert((rows, COLS))],
        out_shape=(jax.ShapeDtypeStruct((2, USED, WIDTH), BF),) * n
        + (jax.ShapeDtypeStruct((2, rows, COLS), BF),),
        scratch_shapes=[pltpu.VMEM((rows, WIDTH), BF)],
        compiler_params=params(48, 1),
        cost_estimate=cost(4 * 10**9, 18 * 10**6),
        name="backward",
    )(*blocks, wd, bm, a, wg, wu, mask, a1, a2)
    return res[:n], res[n]


def grads_kernel(*refs):
    blocks, (hid, low, bl0, bl1, ga, gb, ys) = refs[:NB], refs[NB:]
    stack(ys, blocks, WIDTH)
    half = NB // 2 * PITCH
    gb[0] = dot(low[0], ys[...], 0, 0)
    ga[0] = (dot(hid[0, :half], bl0[0], 0, 0) + dot(hid[0, half:], bl1[0], 0, 0)).astype(BF)


def grads(blocks, hid, low, bl0, bl1):
    rows = NB * PITCH
    return pl.pallas_call(
        grads_kernel,
        grid=(2,),
        in_specs=[per_expert((USED, WIDTH))] * NB
        + [
            per_expert((rows, HID)),
            per_expert((rows, COLS)),
            per_expert((rows // 2, COLS)),
            per_expert((rows // 2, COLS)),
        ],
        out_specs=[per_expert((HID, COLS)), per_expert((COLS, WIDTH))],
        out_shape=(
            jax.ShapeDtypeStruct((2, HID, COLS), BF),
            jax.ShapeDtypeStruct((2, COLS, WIDTH), F32),
        ),
        scratch_shapes=[pltpu.VMEM((rows, WIDTH), BF)],
        compiler_params=params(40, 1),
        cost_estimate=cost(10**9, 10 * 10**6),
        name="grads",
    )(*blocks, hid, low, bl0, bl1)


def combine_kernel(o_ref, *refs):
    blocks, outs, bs = refs[:NB], refs[NB : NB + SIDE], refs[NB + SIDE]
    pad = jnp.zeros((PITCH - USED, WIDTH), BF)
    for b in range(NB):
        for j in range(2):
            at = (2 * b + j) * PITCH
            bs[at + 64 : at + PITCH, :] = jnp.zeros((PITCH - 64, WIDTH), BF)
            bs[at : at + USED, :] = blocks[b][j]

    def step(n, carry):
        cols = pl.ds(pl.multiple_of(n * 256, 256), 256)
        total = dot(o_ref[...], bs[:, cols], 0, 0)
        for d in range(SIDE):
            outs[d][:, cols] = total[d * TOK : (d + 1) * TOK].astype(outs[d].dtype)
        return carry

    lax.fori_loop(0, WIDTH // 256, step, 0)


def combine(onehot, blocks):
    return pl.pallas_call(
        combine_kernel,
        out_shape=(jax.ShapeDtypeStruct((TOK, WIDTH), F32),)
        + (jax.ShapeDtypeStruct((TOK, WIDTH), BF),) * (SIDE - 1),
        scratch_shapes=[pltpu.VMEM((NB * 2 * PITCH, WIDTH), BF)],
        compiler_params=params(40),
        cost_estimate=cost(3 * 10**9, 10 * 10**6),
        name="combine",
    )(onehot, *blocks)


def send(block, pairs):
    return lax.ppermute(block, "expert", pairs)


def send_all(blocks):
    return [
        block if dest == (0, 0) else send(block, cross_pairs(*dest))
        for block, dest in zip(blocks, DESTS)
    ]


def on_device(tokens, dy, routes, weight, tenant, wg, wu, wd, a, bm):
    meta = jnp.concatenate(
        [routes.astype(BF), weight, tenant.astype(BF)[:, None], jnp.zeros((TOK, META - 17), BF)],
        axis=1,
    )
    wide = jnp.concatenate([tokens, meta], axis=1)
    x_line = [wide] + [send(wide, line_pairs(d)) for d in range(1, SIDE)]
    onehot, weighted, x_out = gather_x(x_line)
    dy_line = [dy] + [send(dy, line_pairs(d)) for d in range(1, SIDE)]
    x_in = send_all(x_out)
    dy_in = send_all(gather_dy(weighted, dy_line))
    hid, low, mask, a1, a2 = forward(x_in, wg, wu, a)
    half = NB // 2
    back0, bl0 = backward(0, dy_in[:half], wd, bm, a, wg, wu, mask, a1, a2)
    back1, bl1 = backward(1, dy_in[half:], wd, bm, a, wg, wu, mask, a1, a2)
    returned = [
        block if dest == (0, 0) else send(block, back_pairs(cross_pairs(*dest)))
        for block, dest in zip(list(back0) + list(back1), DESTS)
    ]
    ga, gb = grads(dy_in, hid, low, bl0, bl1)
    parts = combine(onehot, returned)
    total = parts[0]
    for d in range(1, SIDE):
        total = total + send(parts[d], back_pairs(line_pairs(d))).astype(F32)
    gb = lax.psum_scatter(gb, "dp", scatter_dimension=2, tiled=True)
    ga = jnp.sum(lax.all_gather(ga, "dp").astype(F32), axis=0)
    return total.astype(BF), ga, gb


def solution(mesh):
    spread = P(("dp", "expert"), None)
    experts = P("expert", None, None)
    return jax.shard_map(
        on_device,
        mesh=mesh,
        in_specs=(spread, spread, spread, spread, P(("dp", "expert"))) + (experts,) * 5,
        out_specs=(spread, experts, P("expert", None, "dp")),
        check_vma=False,
    )
```

```python
import jax
import jax.numpy as jnp
from jax import lax
from jax.experimental import pallas as pl
from jax.experimental.pallas import tpu as pltpu
from jax.sharding import PartitionSpec as P

SIDE = 4
TOK = 128
WIDTH = 2048
HID = 384
COLS = 128
RANK = 16
TOP = 8
CAP = 18
EXPERTS = 64
META = 128
WIDE = WIDTH + META
FULL = WIDE + WIDTH
LINE = SIDE * TOK
USED = SIDE * CAP
PITCH = 80
NEAR = ((0, 0), (1, 0), (3, 0), (1, 1), (3, 1))
FAR = ((0, 1), (2, 0), (2, 1))
DESTS = NEAR + FAR
GROUPS = (NEAR, FAR)
NB = len(DESTS)
BF = jnp.bfloat16
F32 = jnp.float32
MIB = 1024 * 1024
LIMIT = 60
SHADOWS = ("backward_far", "combine_near", "combine_far")
GRAD = BF


def place(y, x, c):
    return ((y % SIDE) * SIDE + x % SIDE) * 2 + c


def all_places():
    return [(y, x, c) for y in range(SIDE) for x in range(SIDE) for c in range(2)]


def line_pairs(d):
    return [
        (place(y, x, c), place(y + d, x, c) if c == 0 else place(y, x + d, c))
        for y, x, c in all_places()
    ]


def cross_pairs(d, other):
    return [
        (place(y, x, c), place(y, x + d, c ^ other) if c == 0 else place(y + d, x, c ^ other))
        for y, x, c in all_places()
    ]


def back_pairs(pairs):
    return [(b, a) for a, b in pairs]


def params(mib, dims=0):
    return pltpu.CompilerParams(
        vmem_limit_bytes=mib * MIB,
        dimension_semantics=("arbitrary",) * dims if dims else None,
    )


LONG = pl.CostEstimate(flops=3 * 10**10, bytes_accessed=10**8, transcendentals=0)
HINT = pl.CostEstimate(flops=10**6, bytes_accessed=10**5, transcendentals=0)


def iota(shape, dim):
    return lax.broadcasted_iota(jnp.int32, shape, dim)


def dot(a, b, ca=1, cb=0):
    return lax.dot_general(a, b, (((ca,), (cb,)), ((), ())), preferred_element_type=F32)


def build_onehots(metas, dests, o_ref, ow_ref):
    me = lax.axis_index("expert")
    c, x, y = me & 1, (me >> 1) & 3, me >> 3
    ids = iota((EXPERTS, TOK), 0).astype(F32)
    tri = (iota((TOK, TOK), 0) <= iota((TOK, TOK), 1)).astype(F32).astype(BF)
    ranks, weights = [], []
    for meta in metas:
        flipped = meta.astype(F32).T
        named = jnp.zeros((EXPERTS, TOK), F32)
        weight = jnp.zeros((EXPERTS, TOK), F32)
        for k in range(TOP):
            hit = flipped[k : k + 1, :] == ids
            named = named + jnp.where(hit, 1.0, 0.0)
            weight = weight + jnp.where(hit, flipped[TOP + k : TOP + k + 1, :], 0.0)
        rank = dot(named.astype(BF), tri) * named
        ranks.append(rank.astype(BF))
        weights.append(weight.astype(BF))
    rank = jnp.concatenate(ranks, axis=1)
    weight = jnp.concatenate(weights, axis=1)
    rows = 2 * PITCH
    r = iota((rows, LINE), 0)
    j = (r >= PITCH).astype(jnp.int32)
    rr = r - PITCH * j
    d = sum((rr >= CAP * i).astype(jnp.int32) for i in range(1, SIDE))
    want = jnp.where((rr < USED) & ((iota((rows, LINE), 1) >> 7) == d), rr - CAP * d + 1, -1)
    want = want.astype(F32)
    col = iota((rows, EXPERTS), 1) - (iota((rows, EXPERTS), 0) >= PITCH).astype(jnp.int32)
    for b, (step, other) in enumerate(dests):
        along_x = (y << 4) + (((x + step) & 3) << 2)
        along_y = (((y + step) & 3) << 4) + (x << 2)
        base = jnp.where(c == 0, along_x, along_y) + ((c ^ other) << 1)
        sel = (col == base).astype(F32).astype(BF)
        hit = dot(sel, rank) == want
        o_ref[b * rows : (b + 1) * rows, :] = jnp.where(hit, 1.0, 0.0).astype(BF)
        ow_ref[b * rows : (b + 1) * rows, :] = jnp.where(hit, dot(sel, weight), 0.0).astype(BF)


def widen_kernel(tokens, routes, weight, tenant, out):
    out[:, :WIDTH] = tokens[...]
    flipped = jnp.concatenate(
        [
            routes[...].astype(F32),
            weight[...].astype(F32),
            jnp.broadcast_to(tenant[...].astype(F32), (8, TOK)),
            jnp.zeros((META - 24, TOK), F32),
        ],
        axis=0,
    )
    out[:, WIDTH:] = flipped.T.astype(BF)


def widen(tokens, routes, weight, tenant):
    return pl.pallas_call(
        widen_kernel,
        out_shape=jax.ShapeDtypeStruct((TOK, WIDE), BF),
        compiler_params=params(LIMIT),
        cost_estimate=HINT,
        name="widen",
    )(tokens, routes.T, weight.T, tenant[None, :])


ANY = pl.BlockSpec(memory_space=pl.ANY)


class Mover:
    def __init__(self, sems):
        self.sems, self.used = sems, 0

    def start(self, src, dst):
        copy = pltpu.make_async_copy(src, dst, self.sems.at[self.used])
        self.used += 1
        copy.start()
        return copy


def wait(copies):
    for copy in copies:
        copy.wait()


def manual(kernel, ins, outs, scratch, copies, name, aliases=None):
    return pl.pallas_call(
        kernel,
        in_specs=[ANY] * len(ins),
        out_specs=[ANY] * len(outs),
        out_shape=[jax.ShapeDtypeStruct(shape, kind) for shape, kind in outs],
        scratch_shapes=[pltpu.VMEM(shape, kind) for shape, kind in scratch]
        + [pltpu.SemaphoreType.DMA((copies,))],
        compiler_params=params(LIMIT),
        input_output_aliases=aliases or {},
        cost_estimate=LONG if name in SHADOWS else HINT,
        name=name,
    )(*ins)


def index(dests, x_line, after=()):
    shape = (len(dests) * 2 * PITCH, LINE)

    def kernel(*refs):
        o_ref, ow_ref = refs[-2:]
        build_onehots([m[...] for m in refs[:SIDE]], dests, o_ref, ow_ref)

    return pl.pallas_call(
        kernel,
        grid=(1,),
        in_specs=[pl.BlockSpec((TOK, META), lambda i: (0, WIDTH // META))] * SIDE
        + [ANY] * len(after),
        out_specs=[pl.BlockSpec(shape, lambda i: (0, 0))] * 2,
        out_shape=[jax.ShapeDtypeStruct(shape, BF)] * 2,
        compiler_params=params(LIMIT, 1),
        cost_estimate=HINT,
        name="index_near" if dests is NEAR else "index_far",
    )(*x_line, *after)


def gather(onehot, line, into, name, after=()):
    width = line[0].shape[1]
    start = WIDE if into else 0
    n = onehot.shape[0] // (2 * PITCH)
    step = 512
    chunks = [(at, min(step, width - at)) for at in range(0, width, step)]
    scratch = [(onehot.shape, BF), ((LINE, width), BF), ((n, 2, USED, width), BF)]

    def kernel(*refs):
        flat, srcs, dsts, (vo, vs, vb, sems) = refs[0], refs[1 : 1 + SIDE], refs[-n - 4 : -4], refs[-4:]
        mover = Mover(sems)
        one = mover.start(flat, vo)
        loads = []
        for at, size in chunks:
            cols = slice(at, at + size)
            loads.append(
                [
                    mover.start(srcs[i].at[:, cols], vs.at[i * TOK : (i + 1) * TOK, cols])
                    for i in range(SIDE)
                ]
            )
        one.wait()
        stores = []
        for (at, size), load in zip(chunks, loads):
            wait(load)
            cols = slice(at, at + size)
            picked = dot(vo[...], vs[:, cols])
            for b in range(n):
                for j in range(2):
                    row = (2 * b + j) * PITCH
                    vb[b, j, :, cols] = picked[row : row + USED].astype(BF)
            there = slice(start + at, start + at + size)
            stores += [
                mover.start(vb.at[b, :, :, cols], dsts[b].at[:, :, there]) for b in range(n)
            ]
        wait(stores)

    return manual(
        kernel,
        [onehot, *line, *into, *after],
        [((2, USED, FULL), BF)] * n,
        scratch,
        1 + len(chunks) * (SIDE + n),
        name,
        {1 + SIDE + i: i for i in range(len(into))},
    )


def expert(blocks, wg, wu, wd, a, bm, after=()):
    n = len(blocks)
    rows = n * PITCH
    ins = [*blocks, wg, wu, a, bm, wd]
    outs = [((2, USED, WIDTH), BF)] * n
    extra = [((2, HID, COLS), F32), ((2, COLS, WIDTH), F32)]
    scratch = extra + [
        ((2, WIDTH, 2 * HID), BF),
        ((2, HID + COLS, WIDTH), BF),
        (a.shape, BF),
        ((n, 2, USED, FULL), BF),
        ((n, 2, USED, WIDTH), BF),
        ((rows, WIDTH), BF),
        ((rows, WIDTH), BF),
        ((rows, COLS), F32),
    ]

    def kernel(*refs):
        srcs, refs = refs[: len(ins)], refs[len(ins) + len(after) :]
        dsts, refs = refs[: n + len(extra)], refs[n + len(extra) :]
        more, refs = refs[: len(extra)], refs[len(extra) :]
        vgu, vdm, va, raw, res, xs, ys, ts, sems = refs
        sg, su, sa, sm, sd = srcs[n:]
        mover = Mover(sems)
        loads = []
        for j in range(2):
            loads.append([mover.start(srcs[i].at[j], raw.at[i, j]) for i in range(n)])
            loads.append(
                [
                    mover.start(sg.at[j], vgu.at[j, :, :HID]),
                    mover.start(su.at[j], vgu.at[j, :, HID:]),
                ]
            )
            loads.append(
                [
                    mover.start(sd.at[j], vdm.at[j, :HID]),
                    mover.start(sm.at[j], vdm.at[j, HID:]),
                    mover.start(sa.at[j], va.at[j]),
                ]
            )
        stores = []
        column = (iota((rows, COLS), 1) >> 4).astype(F32)
        ts[...] = jnp.zeros_like(ts)
        for ref in (xs, ys):
            for i in range(n):
                ref[i * PITCH + 64 : (i + 1) * PITCH, :] = jnp.zeros((16, WIDTH), BF)
        for j in range(2):
            wait(loads[3 * j])
            for i in range(n):
                at = slice(i * PITCH, i * PITCH + USED)
                xs[at, :] = raw[i, j, :, :WIDTH]
                ts[at, :] = raw[i, j, :, WIDTH:WIDE].astype(F32)
                ys[at, :] = raw[i, j, :, WIDE:]
            x, s = xs[...], ys[...]
            mask = jnp.where(ts[:, 2 * TOP : 2 * TOP + 1] == column, 1.0, 0.0)
            wait(loads[3 * j + 1])
            both = dot(x, vgu[j])
            gate, up = both[:, :HID], both[:, HID:]
            sig = jax.nn.sigmoid(gate)
            act = gate * sig
            hid = (act * up).astype(BF)
            slope = up * sig * (1.0 + gate * (1.0 - sig))
            wait(loads[3 * j + 2])
            both = dot(s, vdm[j], 1, 1)
            bl = (both[:, HID:] * mask).astype(BF)
            dh = both[:, :HID] + dot(bl, va[j], 1, 1)
            slopes = jnp.concatenate([(dh * slope).astype(BF), (dh * act).astype(BF)], axis=1)
            for k in range(WIDTH // 512):
                at = slice(k * 512, (k + 1) * 512)
                back = dot(slopes, vgu[j, at, :], 1, 1)
                for i in range(n):
                    res[i, j, :, at] = back[i * PITCH : i * PITCH + USED].astype(BF)
            stores += [mover.start(res.at[i, j], dsts[i].at[j]) for i in range(n)]
            low = (dot(hid, va[j]) * mask).astype(BF)
            more[0][j] = dot(hid, bl, 0, 0)
            more[1][j] = dot(low, s, 0, 0)
            stores += [mover.start(src.at[j], dst.at[j]) for src, dst in zip(more, dsts[n:])]
        wait(stores)

    res = manual(
        kernel, ins + list(after), outs + extra, scratch, 4 * n + 10 + 2 * len(extra), "expert_near"
    )
    return res[:n], res[n:]


SHARE = WIDTH // 8
PACK = 2 * COLS + HID * COLS * 2 // 8 // SHARE


def unstack(scratch, raw, j, cols):
    for i in range(raw.shape[0]):
        scratch[i * PITCH : i * PITCH + USED, :] = raw[i, j, :, cols]


def clear_pads(scratch):
    for at in range(0, scratch.shape[0], PITCH):
        scratch[at + 64 : at + PITCH, :] = jnp.zeros((16, scratch.shape[1]), scratch.dtype)


def forward_far(blocks, wg, wu, a, bm, before, after=()):
    n = len(blocks)
    rows = n * PITCH
    ins = [*blocks, wg, wu, a, bm, *before]
    kept = [((2, rows, COLS), BF), ((2, rows, HID), F32), ((2, rows, HID), F32)]
    outs = kept + [((8, PACK, SHARE), GRAD)]
    scratch = outs + [
        ((n, 2, USED, FULL), BF),
        ((2, WIDTH, 2 * HID), BF),
        (a.shape, BF),
        (bm.shape, BF),
        (before[0].shape, F32),
        (before[1].shape, F32),
        ((rows, WIDTH), BF),
        ((rows, WIDTH), BF),
        ((rows, COLS), F32),
    ]

    def kernel(*refs):
        srcs, refs = refs[: len(ins)], refs[len(ins) + len(after) :]
        dsts, bufs, refs = refs[:4], refs[4:8], refs[8:]
        raw, vgu, va, vm, ga0, gb0, xs, ys, ts, sems = refs
        sg, su, sa, sm, sga, sgb = srcs[n:]
        mover = Mover(sems)
        loads = []
        for j in range(2):
            loads.append([mover.start(srcs[i].at[j], raw.at[i, j]) for i in range(n)])
            loads.append(
                [
                    mover.start(sg.at[j], vgu.at[j, :, :HID]),
                    mover.start(su.at[j], vgu.at[j, :, HID:]),
                ]
            )
            pairs = ((sa, va), (sm, vm), (sga, ga0), (sgb, gb0))
            loads.append([mover.start(src.at[j], dst.at[j]) for src, dst in pairs])
        column = (iota((rows, COLS), 1) >> 4).astype(F32)
        ts[...] = jnp.zeros_like(ts)
        clear_pads(xs)
        clear_pads(ys)
        stores = []
        out = bufs[3]
        for j in range(2):
            wait(loads[3 * j])
            unstack(xs, raw, j, slice(0, WIDTH))
            unstack(ys, raw, j, slice(WIDE, FULL))
            for i in range(n):
                ts[i * PITCH : i * PITCH + USED, :] = raw[i, j, :, WIDTH:WIDE].astype(F32)
            mask = jnp.where(ts[:, 2 * TOP : 2 * TOP + 1] == column, 1.0, 0.0)
            wait(loads[3 * j + 1])
            both = dot(xs[...], vgu[j])
            gate, up = both[:, :HID], both[:, HID:]
            sig = jax.nn.sigmoid(gate)
            act = gate * sig
            hid = (act * up).astype(BF)
            bufs[1][j] = up * sig * (1.0 + gate * (1.0 - sig))
            bufs[2][j] = act
            wait(loads[3 * j + 2])
            bl = (dot(ys[...], vm[j], 1, 1) * mask).astype(BF)
            bufs[0][j] = bl
            low = (dot(hid, va[j]) * mask).astype(BF)
            gb = (dot(low, ys[...], 0, 0) + gb0[j]).astype(GRAD)
            for k in range(8):
                out[k, j * COLS : (j + 1) * COLS, :] = gb[:, k * SHARE : (k + 1) * SHARE]
            ga = (dot(hid, bl, 0, 0) + ga0[j]).astype(GRAD)
            half = PACK - 2 * COLS
            for k in range(4):
                at = 2 * k * half
                out[4 * j + k, 2 * COLS :, :COLS] = ga[at : at + half]
                out[4 * j + k, 2 * COLS :, COLS:] = ga[at + half : at + 2 * half]
            stores += [mover.start(bufs[k].at[j], dsts[k].at[j]) for k in range(3)]
        stores.append(mover.start(out, dsts[3]))
        wait(stores)

    *kept, packed = manual(
        kernel, ins + list(after), outs, scratch, 2 * (n + 6) + 7, "forward_far"
    )
    return kept, packed


def backward_far(blocks, wd, a, wg, wu, kept, after=()):
    n = len(blocks)
    rows = n * PITCH
    ins = [*blocks, wd, a, *kept, wg, wu]
    outs = [((2, USED, WIDTH), BF)] * n
    scratch = [
        ((n, 2, USED, WIDTH), BF),
        ((n, 2, USED, WIDTH), BF),
        (wd.shape, BF),
        (a.shape, BF),
        (kept[0].shape, BF),
        (kept[1].shape, F32),
        (kept[2].shape, F32),
        ((2, WIDTH, 2 * HID), BF),
        ((rows, WIDTH), BF),
    ]

    def kernel(*refs):
        srcs, refs = refs[: len(ins)], refs[len(ins) + len(after) :]
        dsts, (raw, res, vd, va, vbl, slope, act, vgu, ys, sems) = refs[:n], refs[n:]
        sg, su = srcs[n + 5 :]
        mover = Mover(sems)
        loads = []
        for j in range(2):
            load = [mover.start(srcs[i].at[j, :, WIDE:], raw.at[i, j]) for i in range(n)]
            pairs = zip(srcs[n : n + 5], (vd, va, vbl, slope, act))
            load += [mover.start(src.at[j], dst.at[j]) for src, dst in pairs]
            loads.append(load)
            loads.append(
                [
                    mover.start(sg.at[j], vgu.at[j, :, :HID]),
                    mover.start(su.at[j], vgu.at[j, :, HID:]),
                ]
            )
        clear_pads(ys)
        stores = []
        for j in range(2):
            wait(loads[2 * j])
            unstack(ys, raw, j, slice(0, WIDTH))
            dh = dot(ys[...], vd[j], 1, 1) + dot(vbl[j], va[j], 1, 1)
            slopes = [(dh * slope[j]).astype(BF), (dh * act[j]).astype(BF)]
            slopes = jnp.concatenate(slopes, axis=1)
            wait(loads[2 * j + 1])
            for k in range(WIDTH // 512):
                at = slice(k * 512, (k + 1) * 512)
                back = dot(slopes, vgu[j, at, :], 1, 1)
                for i in range(n):
                    res[i, j, :, at] = back[i * PITCH : i * PITCH + USED].astype(BF)
            stores += [mover.start(res.at[i, j], dsts[i].at[j]) for i in range(n)]
        wait(stores)

    return manual(kernel, ins + list(after), outs, scratch, 4 * n + 14, "backward_far")


def hold(blocks, after):
    n = len(blocks)

    def kernel(*refs):
        pass

    return manual(
        kernel,
        [*blocks, *after],
        [(v.shape, v.dtype) for v in blocks],
        [((8, 128), F32)],
        1,
        "hold",
        {i: i for i in range(n)},
    )


def flip_kernel(o0, o1, t0, t1):
    for src, dst in ((o0, t0), (o1, t1)):
        dst[...] = src[...].astype(F32).T.astype(BF)


def flip(onehots):
    return pl.pallas_call(
        flip_kernel,
        out_shape=[jax.ShapeDtypeStruct(o.shape[::-1], BF) for o in onehots],
        compiler_params=params(LIMIT),
        cost_estimate=HINT,
        name="flip",
    )(*onehots)


def combine(flipped, blocks, before=(), after=()):
    n, last = len(blocks), len(before) > 0
    rows = 2 * PITCH * n
    step = 512
    chunks = [slice(at, at + step) for at in range(0, WIDTH, step)]
    if last:
        outs = [((TOK, WIDTH), F32)] + [((TOK, WIDTH), BF)] * (SIDE - 1)
    else:
        outs = [((LINE, WIDTH), F32)]
    scratch = outs + [((LINE, rows), BF), ((n, 2, USED, WIDTH), BF), ((rows, step), BF)]
    scratch += [((LINE, WIDTH), F32)] * len(before)

    def kernel(*refs):
        flat, srcs = refs[0], refs[1 : 1 + n + len(before)]
        refs = refs[1 + n + len(before) + len(after) :]
        dsts, bufs, refs = refs[: len(outs)], refs[len(outs) : 2 * len(outs)], refs[2 * len(outs) :]
        ot, raw, bs, *prev, sems = refs
        mover = Mover(sems)
        one = mover.start(flat, ot)
        loads = []
        for cols in chunks:
            load = [mover.start(srcs[i].at[:, :, cols], raw.at[i, :, :, cols]) for i in range(n)]
            if last:
                load.append(mover.start(srcs[n].at[:, cols], prev[0].at[:, cols]))
            loads.append(load)
        for i in range(2 * n):
            bs[i * PITCH + 64 : (i + 1) * PITCH, :] = jnp.zeros((16, step), BF)
        one.wait()
        stores = []
        for cols, load in zip(chunks, loads):
            wait(load)
            for i in range(n):
                for j in range(2):
                    at = (2 * i + j) * PITCH
                    bs[at : at + USED, :] = raw[i, j, :, cols]
            total = dot(ot[...], bs[...])
            if last:
                total = total + prev[0][:, cols]
                for d in range(SIDE):
                    bufs[d][:, cols] = total[d * TOK : (d + 1) * TOK].astype(bufs[d].dtype)
            else:
                bufs[0][:, cols] = total
            stores += [mover.start(buf.at[:, cols], dst.at[:, cols]) for buf, dst in zip(bufs, dsts)]
        wait(stores)

    return manual(
        kernel,
        [flipped, *blocks, *before, *after],
        outs,
        scratch,
        1 + len(chunks) * (n + len(before) + len(outs)),
        "combine_far" if last else "combine_near",
    )


def send(block, pairs):
    return lax.ppermute(block, "expert", pairs)


def send_all(blocks, dests):
    return [
        block if dest == (0, 0) else send(block, cross_pairs(*dest))
        for block, dest in zip(blocks, dests)
    ]


def send_back(blocks, dests):
    return [
        block if dest == (0, 0) else send(block, back_pairs(cross_pairs(*dest)))
        for block, dest in zip(blocks, dests)
    ]


def along_line(block):
    return [block] + [send(block, line_pairs(d)) for d in range(1, SIDE)]


def reduce_dp(packed):
    def swap(v):
        return lax.all_to_all(v, "dp", split_axis=0, concat_axis=0, tiled=True)

    total = jnp.sum(swap(packed).astype(F32), axis=0)
    gb = total[: 2 * COLS].reshape(2, COLS, SHARE)
    chunk = total[2 * COLS :]
    chunk = jnp.concatenate([chunk[:, :COLS], chunk[:, COLS:]], axis=0)
    ga = swap(jnp.broadcast_to(chunk[None], (8,) + chunk.shape))
    return ga.reshape(2, HID, COLS), gb


def on_device(tokens, dy, routes, weight, tenant, wg, wu, wd, a, bm):
    x_line = along_line(widen(tokens, routes, weight, tenant))
    dy_line = along_line(dy)
    one0, weighted0 = index(NEAR, x_line)
    near = gather(one0, x_line, (), "gather_x_near")
    near = send_all(gather(weighted0, dy_line, near, "gather_near"), NEAR)
    one1, weighted1 = index(FAR, x_line, after=near[:1])
    far = gather(one1, x_line, (), "gather_x_far")
    far = gather(weighted1, dy_line, far, "gather_far")
    far = hold(far, near[1:4])
    flipped = flip((one0, one1))
    back_near, sums = expert(near, wg, wu, wd, a, bm, after=(far[0], flipped[0]))
    far = send_all(far, FAR)
    kept, packed = forward_far(far, wg, wu, a, bm, sums, after=back_near[:1])
    later = hold(back_near[3:], kept[:1])
    back_near = send_back([*back_near[:3], *later], NEAR)
    back_far = backward_far(far, wd, a, wg, wu, kept, after=back_near)
    back_far = send_back(back_far, FAR)
    ga, gb = reduce_dp(packed)
    (partial,) = combine(flipped[0], back_near)
    parts = combine(flipped[1], back_far, (partial,))
    total = parts[0]
    for d in range(1, SIDE):
        total = total + send(parts[d], back_pairs(line_pairs(d))).astype(F32)
    return total.astype(BF), ga, gb


def solution(mesh):
    spread = P(("dp", "expert"), None)
    experts = P("expert", None, None)
    return jax.shard_map(
        on_device,
        mesh=mesh,
        in_specs=(spread, spread, spread, spread, P(("dp", "expert"))) + (experts,) * 5,
        out_specs=(spread, experts, P("expert", None, "dp")),
        check_vma=False,
    )
```

```python
import jax
import jax.numpy as jnp
from jax import lax
from jax.experimental import pallas as pl
from jax.experimental.pallas import tpu as pltpu
from jax.sharding import PartitionSpec as P

SIDE = 4
TOK = 128
WIDTH = 2048
HID = 384
COLS = 128
RANK = 16
TOP = 8
CAP = 18
EXPERTS = 64
META = 128
WIDE = WIDTH + META
FULL = WIDE + WIDTH
LINE = SIDE * TOK
USED = SIDE * CAP
PITCH = 80
NEAR = ((1, 0), (3, 0), (1, 1), (3, 1), (0, 1), (0, 0))
FAR = ((2, 0), (2, 1))
DESTS = NEAR + FAR
GROUPS = (NEAR, FAR)
NB = len(DESTS)
BF = jnp.bfloat16
F32 = jnp.float32
MIB = 1024 * 1024
LIMIT = 63
SHADOWS = ("backward_far", "combine_near", "combine_far")
GRAD = BF


def place(y, x, c):
    return ((y % SIDE) * SIDE + x % SIDE) * 2 + c


def all_places():
    return [(y, x, c) for y in range(SIDE) for x in range(SIDE) for c in range(2)]


def line_pairs(d):
    return [
        (place(y, x, c), place(y + d, x, c) if c == 0 else place(y, x + d, c))
        for y, x, c in all_places()
    ]


def cross_pairs(d, other):
    return [
        (place(y, x, c), place(y, x + d, c ^ other) if c == 0 else place(y + d, x, c ^ other))
        for y, x, c in all_places()
    ]


def back_pairs(pairs):
    return [(b, a) for a, b in pairs]


def params(mib, dims=0):
    return pltpu.CompilerParams(
        vmem_limit_bytes=mib * MIB,
        dimension_semantics=("arbitrary",) * dims if dims else None,
    )


LONG = pl.CostEstimate(flops=3 * 10**10, bytes_accessed=10**8, transcendentals=0)
HINT = pl.CostEstimate(flops=10**6, bytes_accessed=10**5, transcendentals=0)


def iota(shape, dim):
    return lax.broadcasted_iota(jnp.int32, shape, dim)


def dot(a, b, ca=1, cb=0):
    return lax.dot_general(a, b, (((ca,), (cb,)), ((), ())), preferred_element_type=F32)


def build_onehots(metas, dests, o_ref, ow_ref):
    me = lax.axis_index("expert")
    c, x, y = me & 1, (me >> 1) & 3, me >> 3
    ids = iota((EXPERTS, TOK), 0).astype(F32)
    tri = (iota((TOK, TOK), 0) <= iota((TOK, TOK), 1)).astype(F32).astype(BF)
    ranks, weights = [], []
    for meta in metas:
        flipped = meta.astype(F32).T
        named = jnp.zeros((EXPERTS, TOK), F32)
        weight = jnp.zeros((EXPERTS, TOK), F32)
        for k in range(TOP):
            hit = flipped[k : k + 1, :] == ids
            named = named + jnp.where(hit, 1.0, 0.0)
            weight = weight + jnp.where(hit, flipped[TOP + k : TOP + k + 1, :], 0.0)
        rank = dot(named.astype(BF), tri) * named
        ranks.append(rank.astype(BF))
        weights.append(weight.astype(BF))
    rank = jnp.concatenate(ranks, axis=1)
    weight = jnp.concatenate(weights, axis=1)
    rows = 2 * PITCH
    r = iota((rows, LINE), 0)
    j = (r >= PITCH).astype(jnp.int32)
    rr = r - PITCH * j
    d = sum((rr >= CAP * i).astype(jnp.int32) for i in range(1, SIDE))
    want = jnp.where((rr < USED) & ((iota((rows, LINE), 1) >> 7) == d), rr - CAP * d + 1, -1)
    want = want.astype(F32)
    col = iota((rows, EXPERTS), 1) - (iota((rows, EXPERTS), 0) >= PITCH).astype(jnp.int32)
    for b, (step, other) in enumerate(dests):
        along_x = (y << 4) + (((x + step) & 3) << 2)
        along_y = (((y + step) & 3) << 4) + (x << 2)
        base = jnp.where(c == 0, along_x, along_y) + ((c ^ other) << 1)
        sel = (col == base).astype(F32).astype(BF)
        hit = dot(sel, rank) == want
        o_ref[b * rows : (b + 1) * rows, :] = jnp.where(hit, 1.0, 0.0).astype(BF)
        ow_ref[b * rows : (b + 1) * rows, :] = jnp.where(hit, dot(sel, weight), 0.0).astype(BF)


def widen_kernel(tokens, routes, weight, tenant, out):
    out[:, :WIDTH] = tokens[...]
    flipped = jnp.concatenate(
        [
            routes[...].astype(F32),
            weight[...].astype(F32),
            jnp.broadcast_to(tenant[...].astype(F32), (8, TOK)),
            jnp.zeros((META - 24, TOK), F32),
        ],
        axis=0,
    )
    out[:, WIDTH:] = flipped.T.astype(BF)


def widen(tokens, routes, weight, tenant):
    return pl.pallas_call(
        widen_kernel,
        out_shape=jax.ShapeDtypeStruct((TOK, WIDE), BF),
        compiler_params=params(LIMIT),
        cost_estimate=HINT,
        name="widen",
    )(tokens, routes.T, weight.T, tenant[None, :])


ANY = pl.BlockSpec(memory_space=pl.ANY)


class Mover:
    def __init__(self, sems):
        self.sems, self.used = sems, 0

    def start(self, src, dst):
        copy = pltpu.make_async_copy(src, dst, self.sems.at[self.used])
        self.used += 1
        copy.start()
        return copy


def wait(copies):
    for copy in copies:
        copy.wait()


def manual(kernel, ins, outs, scratch, copies, name, aliases=None):
    return pl.pallas_call(
        kernel,
        in_specs=[ANY] * len(ins),
        out_specs=[ANY] * len(outs),
        out_shape=[jax.ShapeDtypeStruct(shape, kind) for shape, kind in outs],
        scratch_shapes=[pltpu.VMEM(shape, kind) for shape, kind in scratch]
        + [pltpu.SemaphoreType.DMA((copies,))],
        compiler_params=params(LIMIT),
        input_output_aliases=aliases or {},
        cost_estimate=LONG if name in SHADOWS else HINT,
        name=name,
    )(*ins)


def index(dests, x_line, after=()):
    shape = (len(dests) * 2 * PITCH, LINE)

    def kernel(*refs):
        o_ref, ow_ref = refs[-2:]
        build_onehots([m[...] for m in refs[:SIDE]], dests, o_ref, ow_ref)

    return pl.pallas_call(
        kernel,
        grid=(1,),
        in_specs=[pl.BlockSpec((TOK, META), lambda i: (0, WIDTH // META))] * SIDE
        + [ANY] * len(after),
        out_specs=[pl.BlockSpec(shape, lambda i: (0, 0))] * 2,
        out_shape=[jax.ShapeDtypeStruct(shape, BF)] * 2,
        compiler_params=params(LIMIT, 1),
        cost_estimate=HINT,
        name="index_near" if dests is NEAR else "index_far",
    )(*x_line, *after)


def gather(onehot, line, into, name, after=()):
    width = line[0].shape[1]
    start = WIDE if into else 0
    n = onehot.shape[0] // (2 * PITCH)
    step = 512
    chunks = [(at, min(step, width - at)) for at in range(0, width, step)]
    scratch = [(onehot.shape, BF), ((LINE, width), BF), ((n, 2, USED, width), BF)]

    def kernel(*refs):
        flat, srcs, dsts, (vo, vs, vb, sems) = refs[0], refs[1 : 1 + SIDE], refs[-n - 4 : -4], refs[-4:]
        mover = Mover(sems)
        one = mover.start(flat, vo)
        loads = []
        for at, size in chunks:
            cols = slice(at, at + size)
            loads.append(
                [
                    mover.start(srcs[i].at[:, cols], vs.at[i * TOK : (i + 1) * TOK, cols])
                    for i in range(SIDE)
                ]
            )
        one.wait()
        stores = []
        for (at, size), load in zip(chunks, loads):
            wait(load)
            cols = slice(at, at + size)
            picked = dot(vo[...], vs[:, cols])
            for b in range(n):
                for j in range(2):
                    row = (2 * b + j) * PITCH
                    vb[b, j, :, cols] = picked[row : row + USED].astype(BF)
            there = slice(start + at, start + at + size)
            stores += [
                mover.start(vb.at[b, :, :, cols], dsts[b].at[:, :, there]) for b in range(n)
            ]
        wait(stores)

    return manual(
        kernel,
        [onehot, *line, *into, *after],
        [((2, USED, FULL), BF)] * n,
        scratch,
        1 + len(chunks) * (SIDE + n),
        name,
        {1 + SIDE + i: i for i in range(len(into))},
    )


def expert(blocks, wg, wu, wd, a, bm, after=()):
    n = len(blocks)
    rows = n * PITCH
    ins = [*blocks, wg, wu, a, bm, wd]
    outs = [((2, USED, WIDTH), BF)] * n
    extra = [((2, HID, COLS), F32), ((2, COLS, WIDTH), F32)]
    scratch = extra + [
        ((2, WIDTH, 2 * HID), BF),
        ((2, HID + COLS, WIDTH), BF),
        (a.shape, BF),
        ((n, 2, USED, FULL), BF),
        ((n, 2, USED, WIDTH), BF),
        ((rows, WIDTH), BF),
        ((rows, WIDTH), BF),
        ((rows, COLS), F32),
    ]

    def kernel(*refs):
        srcs, refs = refs[: len(ins)], refs[len(ins) + len(after) :]
        dsts, refs = refs[: n + len(extra)], refs[n + len(extra) :]
        more, refs = refs[: len(extra)], refs[len(extra) :]
        vgu, vdm, va, raw, res, xs, ys, ts, sems = refs
        sg, su, sa, sm, sd = srcs[n:]
        mover = Mover(sems)
        loads = []
        for j in range(2):
            loads.append([mover.start(srcs[i].at[j], raw.at[i, j]) for i in range(n)])
            loads.append(
                [
                    mover.start(sg.at[j], vgu.at[j, :, :HID]),
                    mover.start(su.at[j], vgu.at[j, :, HID:]),
                ]
            )
            loads.append(
                [
                    mover.start(sd.at[j], vdm.at[j, :HID]),
                    mover.start(sm.at[j], vdm.at[j, HID:]),
                    mover.start(sa.at[j], va.at[j]),
                ]
            )
        stores = []
        column = (iota((rows, COLS), 1) >> 4).astype(F32)
        ts[...] = jnp.zeros_like(ts)
        for ref in (xs, ys):
            for i in range(n):
                ref[i * PITCH + 64 : (i + 1) * PITCH, :] = jnp.zeros((16, WIDTH), BF)
        for j in range(2):
            wait(loads[3 * j])
            for i in range(n):
                at = slice(i * PITCH, i * PITCH + USED)
                xs[at, :] = raw[i, j, :, :WIDTH]
                ts[at, :] = raw[i, j, :, WIDTH:WIDE].astype(F32)
                ys[at, :] = raw[i, j, :, WIDE:]
            x, s = xs[...], ys[...]
            mask = jnp.where(ts[:, 2 * TOP : 2 * TOP + 1] == column, 1.0, 0.0)
            wait(loads[3 * j + 1])
            both = dot(x, vgu[j])
            gate, up = both[:, :HID], both[:, HID:]
            sig = jax.nn.sigmoid(gate)
            act = gate * sig
            hid = (act * up).astype(BF)
            slope = up * sig * (1.0 + gate * (1.0 - sig))
            wait(loads[3 * j + 2])
            both = dot(s, vdm[j], 1, 1)
            bl = (both[:, HID:] * mask).astype(BF)
            dh = both[:, :HID] + dot(bl, va[j], 1, 1)
            slopes = jnp.concatenate([(dh * slope).astype(BF), (dh * act).astype(BF)], axis=1)
            for k in range(WIDTH // 512):
                at = slice(k * 512, (k + 1) * 512)
                back = dot(slopes, vgu[j, at, :], 1, 1)
                for i in range(n):
                    res[i, j, :, at] = back[i * PITCH : i * PITCH + USED].astype(BF)
            stores += [mover.start(res.at[i, j], dsts[i].at[j]) for i in range(n)]
            low = (dot(hid, va[j]) * mask).astype(BF)
            more[0][j] = dot(hid, bl, 0, 0)
            more[1][j] = dot(low, s, 0, 0)
            stores += [mover.start(src.at[j], dst.at[j]) for src, dst in zip(more, dsts[n:])]
        wait(stores)

    res = manual(
        kernel, ins + list(after), outs + extra, scratch, 4 * n + 10 + 2 * len(extra), "expert_near"
    )
    return res[:n], res[n:]


SHARE = WIDTH // 8
PACK = 2 * COLS + HID * COLS * 2 // 8 // SHARE


def unstack(scratch, raw, j, cols):
    for i in range(raw.shape[0]):
        scratch[i * PITCH : i * PITCH + USED, :] = raw[i, j, :, cols]


def clear_pads(scratch):
    for at in range(0, scratch.shape[0], PITCH):
        scratch[at + 64 : at + PITCH, :] = jnp.zeros((16, scratch.shape[1]), scratch.dtype)


def forward_far(blocks, wg, wu, a, bm, before, after=()):
    n = len(blocks)
    rows = n * PITCH
    ins = [*blocks, wg, wu, a, bm, *before]
    kept = [((2, rows, COLS), BF), ((2, rows, HID), F32), ((2, rows, HID), F32)]
    outs = kept + [((8, PACK, SHARE), GRAD)]
    scratch = outs + [
        ((n, 2, USED, FULL), BF),
        ((2, WIDTH, 2 * HID), BF),
        (a.shape, BF),
        (bm.shape, BF),
        (before[0].shape, F32),
        (before[1].shape, F32),
        ((rows, WIDTH), BF),
        ((rows, WIDTH), BF),
        ((rows, COLS), F32),
    ]

    def kernel(*refs):
        srcs, refs = refs[: len(ins)], refs[len(ins) + len(after) :]
        dsts, bufs, refs = refs[:4], refs[4:8], refs[8:]
        raw, vgu, va, vm, ga0, gb0, xs, ys, ts, sems = refs
        sg, su, sa, sm, sga, sgb = srcs[n:]
        mover = Mover(sems)
        loads = []
        for j in range(2):
            loads.append([mover.start(srcs[i].at[j], raw.at[i, j]) for i in range(n)])
            loads.append(
                [
                    mover.start(sg.at[j], vgu.at[j, :, :HID]),
                    mover.start(su.at[j], vgu.at[j, :, HID:]),
                ]
            )
            pairs = ((sa, va), (sm, vm), (sga, ga0), (sgb, gb0))
            loads.append([mover.start(src.at[j], dst.at[j]) for src, dst in pairs])
        column = (iota((rows, COLS), 1) >> 4).astype(F32)
        ts[...] = jnp.zeros_like(ts)
        clear_pads(xs)
        clear_pads(ys)
        stores = []
        out = bufs[3]
        for j in range(2):
            wait(loads[3 * j])
            unstack(xs, raw, j, slice(0, WIDTH))
            unstack(ys, raw, j, slice(WIDE, FULL))
            for i in range(n):
                ts[i * PITCH : i * PITCH + USED, :] = raw[i, j, :, WIDTH:WIDE].astype(F32)
            mask = jnp.where(ts[:, 2 * TOP : 2 * TOP + 1] == column, 1.0, 0.0)
            wait(loads[3 * j + 1])
            both = dot(xs[...], vgu[j])
            gate, up = both[:, :HID], both[:, HID:]
            sig = jax.nn.sigmoid(gate)
            act = gate * sig
            hid = (act * up).astype(BF)
            bufs[1][j] = up * sig * (1.0 + gate * (1.0 - sig))
            bufs[2][j] = act
            wait(loads[3 * j + 2])
            bl = (dot(ys[...], vm[j], 1, 1) * mask).astype(BF)
            bufs[0][j] = bl
            low = (dot(hid, va[j]) * mask).astype(BF)
            gb = (dot(low, ys[...], 0, 0) + gb0[j]).astype(GRAD)
            for k in range(8):
                out[k, j * COLS : (j + 1) * COLS, :] = gb[:, k * SHARE : (k + 1) * SHARE]
            ga = (dot(hid, bl, 0, 0) + ga0[j]).astype(GRAD)
            half = PACK - 2 * COLS
            for k in range(4):
                at = 2 * k * half
                out[4 * j + k, 2 * COLS :, :COLS] = ga[at : at + half]
                out[4 * j + k, 2 * COLS :, COLS:] = ga[at + half : at + 2 * half]
            stores += [mover.start(bufs[k].at[j], dsts[k].at[j]) for k in range(3)]
        stores.append(mover.start(out, dsts[3]))
        wait(stores)

    *kept, packed = manual(
        kernel, ins + list(after), outs, scratch, 2 * (n + 6) + 7, "forward_far"
    )
    return kept, packed


def backward_far(blocks, wd, a, wg, wu, kept, after=()):
    n = len(blocks)
    rows = n * PITCH
    ins = [*blocks, wd, a, *kept, wg, wu]
    outs = [((2, USED, WIDTH), BF)] * n
    scratch = [
        ((n, 2, USED, WIDTH), BF),
        ((n, 2, USED, WIDTH), BF),
        (wd.shape, BF),
        (a.shape, BF),
        (kept[0].shape, BF),
        (kept[1].shape, F32),
        (kept[2].shape, F32),
        ((2, WIDTH, 2 * HID), BF),
        ((rows, WIDTH), BF),
    ]

    def kernel(*refs):
        srcs, refs = refs[: len(ins)], refs[len(ins) + len(after) :]
        dsts, (raw, res, vd, va, vbl, slope, act, vgu, ys, sems) = refs[:n], refs[n:]
        sg, su = srcs[n + 5 :]
        mover = Mover(sems)
        loads = []
        for j in range(2):
            load = [mover.start(srcs[i].at[j, :, WIDE:], raw.at[i, j]) for i in range(n)]
            pairs = zip(srcs[n : n + 5], (vd, va, vbl, slope, act))
            load += [mover.start(src.at[j], dst.at[j]) for src, dst in pairs]
            loads.append(load)
            loads.append(
                [
                    mover.start(sg.at[j], vgu.at[j, :, :HID]),
                    mover.start(su.at[j], vgu.at[j, :, HID:]),
                ]
            )
        clear_pads(ys)
        stores = []
        for j in range(2):
            wait(loads[2 * j])
            unstack(ys, raw, j, slice(0, WIDTH))
            dh = dot(ys[...], vd[j], 1, 1) + dot(vbl[j], va[j], 1, 1)
            slopes = [(dh * slope[j]).astype(BF), (dh * act[j]).astype(BF)]
            slopes = jnp.concatenate(slopes, axis=1)
            wait(loads[2 * j + 1])
            for k in range(WIDTH // 512):
                at = slice(k * 512, (k + 1) * 512)
                back = dot(slopes, vgu[j, at, :], 1, 1)
                for i in range(n):
                    res[i, j, :, at] = back[i * PITCH : i * PITCH + USED].astype(BF)
            stores += [mover.start(res.at[i, j], dsts[i].at[j]) for i in range(n)]
        wait(stores)

    return manual(kernel, ins + list(after), outs, scratch, 4 * n + 14, "backward_far")


def hold(blocks, after):
    n = len(blocks)

    def kernel(*refs):
        pass

    return manual(
        kernel,
        [*blocks, *after],
        [(v.shape, v.dtype) for v in blocks],
        [((8, 128), F32)],
        1,
        "hold",
        {i: i for i in range(n)},
    )


def flip_kernel(o0, o1, t0, t1):
    for src, dst in ((o0, t0), (o1, t1)):
        dst[...] = src[...].astype(F32).T.astype(BF)


def flip(onehots):
    return pl.pallas_call(
        flip_kernel,
        out_shape=[jax.ShapeDtypeStruct(o.shape[::-1], BF) for o in onehots],
        compiler_params=params(LIMIT),
        cost_estimate=HINT,
        name="flip",
    )(*onehots)


def combine(flipped, blocks, before=(), after=()):
    n, last = len(blocks), len(before) > 0
    rows = 2 * PITCH * n
    step = 512
    chunks = [slice(at, at + step) for at in range(0, WIDTH, step)]
    if last:
        outs = [((TOK, WIDTH), F32)] + [((TOK, WIDTH), BF)] * (SIDE - 1)
    else:
        outs = [((LINE, WIDTH), F32)]
    scratch = outs + [((LINE, rows), BF), ((n, 2, USED, WIDTH), BF), ((rows, step), BF)]
    scratch += [((LINE, WIDTH), F32)] * len(before)

    def kernel(*refs):
        flat, srcs = refs[0], refs[1 : 1 + n + len(before)]
        refs = refs[1 + n + len(before) + len(after) :]
        dsts, bufs, refs = refs[: len(outs)], refs[len(outs) : 2 * len(outs)], refs[2 * len(outs) :]
        ot, raw, bs, *prev, sems = refs
        mover = Mover(sems)
        one = mover.start(flat, ot)
        loads = []
        for cols in chunks:
            load = [mover.start(srcs[i].at[:, :, cols], raw.at[i, :, :, cols]) for i in range(n)]
            if last:
                load.append(mover.start(srcs[n].at[:, cols], prev[0].at[:, cols]))
            loads.append(load)
        for i in range(2 * n):
            bs[i * PITCH + 64 : (i + 1) * PITCH, :] = jnp.zeros((16, step), BF)
        one.wait()
        stores = []
        for cols, load in zip(chunks, loads):
            wait(load)
            for i in range(n):
                for j in range(2):
                    at = (2 * i + j) * PITCH
                    bs[at : at + USED, :] = raw[i, j, :, cols]
            total = dot(ot[...], bs[...])
            if last:
                total = total + prev[0][:, cols]
                for d in range(SIDE):
                    bufs[d][:, cols] = total[d * TOK : (d + 1) * TOK].astype(bufs[d].dtype)
            else:
                bufs[0][:, cols] = total
            stores += [mover.start(buf.at[:, cols], dst.at[:, cols]) for buf, dst in zip(bufs, dsts)]
        wait(stores)

    return manual(
        kernel,
        [flipped, *blocks, *before, *after],
        outs,
        scratch,
        1 + len(chunks) * (n + len(before) + len(outs)),
        "combine_far" if last else "combine_near",
    )


def send(block, pairs):
    return lax.ppermute(block, "expert", pairs)


def send_all(blocks, dests):
    return [
        block if dest == (0, 0) else send(block, cross_pairs(*dest))
        for block, dest in zip(blocks, dests)
    ]


def send_back(blocks, dests):
    return [
        block if dest == (0, 0) else send(block, back_pairs(cross_pairs(*dest)))
        for block, dest in zip(blocks, dests)
    ]


def along_line(block):
    return [block] + [send(block, line_pairs(d)) for d in range(1, SIDE)]


def unpack_kernel(parts, gb, spread):
    total = jnp.sum(parts[...].astype(F32), axis=0)
    gb[...] = total[: 2 * COLS]
    half = PACK - 2 * COLS
    for i in range(8):
        spread[i, :half] = total[2 * COLS :, :COLS]
        spread[i, half:] = total[2 * COLS :, COLS:]


def reduce_dp(packed):
    def swap(v):
        return lax.all_to_all(v, "dp", split_axis=0, concat_axis=0, tiled=True)

    gb, spread = pl.pallas_call(
        unpack_kernel,
        out_shape=[
            jax.ShapeDtypeStruct((2 * COLS, SHARE), F32),
            jax.ShapeDtypeStruct((8, 2 * (PACK - 2 * COLS), COLS), F32),
        ],
        compiler_params=params(LIMIT),
        cost_estimate=HINT,
        name="unpack",
    )(swap(packed))
    return swap(spread).reshape(2, HID, COLS), gb.reshape(2, COLS, SHARE)


def on_device(tokens, dy, routes, weight, tenant, wg, wu, wd, a, bm):
    x_line = along_line(widen(tokens, routes, weight, tenant))
    dy_line = along_line(dy)
    one0, weighted0 = index(NEAR, x_line)
    near = gather(one0, x_line, (), "gather_x_near")
    near = send_all(gather(weighted0, dy_line, near, "gather_near"), NEAR)
    one1, weighted1 = index(FAR, x_line, after=near[:1])
    far = gather(one1, x_line, (), "gather_x_far")
    far = gather(weighted1, dy_line, far, "gather_far")
    far = hold(far, near[:4])
    flipped = flip((one0, one1))
    back_near, sums = expert(near, wg, wu, wd, a, bm, after=(far[0], flipped[0]))
    far = send_all(far, FAR)
    kept, packed = forward_far(far, wg, wu, a, bm, sums, after=back_near[:1])
    later = hold(back_near[2:4], kept[:1])
    back_near = send_back([*back_near[:2], *later, *back_near[4:]], NEAR)
    back_far = backward_far(far, wd, a, wg, wu, kept)
    back_far = send_back(back_far, FAR)
    ga, gb = reduce_dp(packed)
    (partial,) = combine(flipped[0], back_near)
    parts = combine(flipped[1], back_far, (partial,))
    total = parts[0]
    for d in range(1, SIDE):
        total = total + send(parts[d], back_pairs(line_pairs(d))).astype(F32)
    return total.astype(BF), ga, gb


def solution(mesh):
    spread = P(("dp", "expert"), None)
    experts = P("expert", None, None)
    return jax.shard_map(
        on_device,
        mesh=mesh,
        in_specs=(spread, spread, spread, spread, P(("dp", "expert"))) + (experts,) * 5,
        out_specs=(spread, experts, P("expert", None, "dp")),
        check_vma=False,
    )
```
